32 devices in a mesh: rep: 4 (over y, x), ep: 8 (over z, core).
Axes of the slice: x: 2, y: 2, z: 4, core: 2. Of those that a mesh axis runs over, the one named last changes fastest.
Arguments:
- tokens: bfloat16 [1024, 2048], P('ep', 'rep'), may hold values from -6 to 6
- out_grad: bfloat16 [1024, 2048], P('ep', 'rep'), may hold values from -6 to 6
- expert_ids: int32 [1024, 8], P('ep'), may hold values from 0 to 127, all different within a row; in each aligned block of 128 rows (0 to 127, 128 to 255, ...) at most 9 rows name the same one
- route_weight: bfloat16 [1024, 8], P('ep'), may hold values from 0.019897461 to 0.29882812
- w_gate: bfloat16 [128, 2048, 640], P('ep', 'rep'), may hold values from -0.125 to 0.125
- w_up: bfloat16 [128, 2048, 640], P('ep', 'rep'), may hold values from -0.125 to 0.125
- w_down: bfloat16 [128, 640, 2048], P('ep', None, 'rep'), may hold values from -0.25 to 0.25
Outputs:
- token_grad: bfloat16 [1024, 2048], P('ep', 'rep')
- grad_gate: bfloat16 [128, 2048, 640], P('ep', 'rep')
- grad_up: bfloat16 [128, 2048, 640], P('ep', 'rep')
- grad_down: bfloat16 [128, 640, 2048], P('ep', None, 'rep')
The draws below stay inside these ranges and needn't reach their ends.
Inputs may be any that keep to these rules, and one draw needn't show every extreme that they name: `expert_ids`: each token picks 8 different experts. Among the 128 tokens of one index of ep no expert is picked by more than 9 tokens, and in every draw some expert is picked by exactly 9 tokens of some such index.
All inputs are finite; a program needn't handle non-finite values.
Results may differ from the reference program's by a relative error of at most 0.024.
Values may be sent and summed in bfloat16 or wider, within the bound.
A program may use at most 128 MiB of HBM per device.

```python
import math
import jax
import jax.numpy as jnp
import numpy as np
from jax import lax

D = 2048
E = 128
TOP = 8
FFW = 640
TOK_DEV = 128
TOKENS = 1024
CAP = 9
N_REP = 4
N_EP = 8


def levels(own_key, dims, shards, smallest, largest):
    level, own = 1.0, jax.random.fold_in(own_key, 6)
    for dim, parts in shards:
        heights = jnp.exp(jax.random.uniform(jax.random.fold_in(own, dim), (parts,), jnp.float32, smallest / len(shards), largest / len(shards)))
        level = level * jnp.repeat(heights, dims[dim] // parts).reshape([-1 if axis == dim else 1 for axis in range(len(dims))])
    return level


def shared_out(own_key, own, number, rows, amount, top, most, lean):
    order = jax.random.permutation(own_key, amount)
    crowded, ordinary = shares(amount, rows * top, most, lean, True), shares(amount, rows * top, most, lean, False)
    places = jnp.arange(amount)

    def named(tallies, offset_by):
        used = int((tallies > 0).sum())
        fixed = max(1, used // 4)
        shifted = fixed + (places - fixed + offset_by * (used - fixed)) % max(1, amount - fixed)
        return jnp.zeros((amount,), jnp.int32).at[order[jnp.where(places < fixed, places, shifted)]].set(jnp.asarray(tallies, jnp.int32))

    tallies = jnp.where(number % 4 == 0, named(crowded, number // 4), named(ordinary, number - number // 4 - 1))
    mixed = jax.random.permutation(jax.random.fold_in(own, 3), amount)
    source_of, taker = mixed[0:amount // 2 * 2:2], mixed[1:amount // 2 * 2:2]
    margin = jnp.minimum(tallies[source_of] - 1, most - tallies[taker]) // 2
    margin = jnp.where((source_of == order[0]) | (taker == order[0]) | (tallies[taker] == 0), 0, jnp.maximum(margin, 0))
    shifted = jax.random.randint(jax.random.fold_in(own, 4), (amount // 2,), 0, 1 << 20) % (margin + 1)
    tallies = tallies.at[source_of].add(-shifted).at[taker].add(shifted)
    members = jnp.searchsorted(jnp.cumsum(tallies), jnp.arange(rows * top), side="right").astype(jnp.int32)
    grid = members.reshape(top, rows).T
    grid = grid[jax.random.permutation(jax.random.fold_in(own, 1), rows)]
    offset_by = jax.random.randint(jax.random.fold_in(own, 2), (rows, 1), 0, top)
    return jnp.take_along_axis(grid, (jnp.arange(top)[None, :] + offset_by) % top, axis=1)


def shares(amount, total, limit, slope, full):
    loads = [(1 << 20) // math.isqrt(standing ** slope) + 1 for standing in range(1, amount + 1)]
    largest = limit if full else min(limit, max(-(-total // amount), total * loads[0] // sum(loads)))
    least = 1 if total - largest >= amount - 1 else 0
    holding, spare = [largest] + [least] * (amount - 1), total - largest - least * (amount - 1)
    while spare > 0:
        candidates = [i for i in range(1, amount) if holding[i] < largest] or [i for i in range(1, amount) if holding[i] < limit]
        whole, left = sum([loads[i] for i in candidates]), spare
        for i in candidates:
            extra = min(limit - holding[i], max(1, left * loads[i] // whole), spare)
            holding[i] = holding[i] + extra
            spare = spare - extra
    return np.array(holding)


def normal_values(rng, shape, scale, most, cuts=(), held_as=jnp.bfloat16):
    entries = scale * jax.random.normal(rng, shape, jnp.float32)
    if cuts:
        entries = entries * levels(rng, shape, cuts, -0.22, 0.18)
    return jnp.clip(entries, -most, most).astype(held_as)


def setup_inputs(seed: int = 0) -> dict:
    keys = jax.random.split(jax.random.key(seed), 8)
    tokens = normal_values(keys[0], (TOKENS, D), 1.0, 6.0, ((0, 8), (1, 4)))
    out_grad = normal_values(keys[1], (TOKENS, D), 1.0, 6.0, ((0, 8), (1, 4)))
    expert_ids_keys = jax.random.split(jax.random.fold_in(keys[2], 1), TOKENS // TOK_DEV)
    expert_ids_turns = jax.random.permutation(jax.random.fold_in(keys[2], 3), TOKENS // TOK_DEV)
    expert_ids = jax.vmap(lambda own, number: shared_out(jax.random.fold_in(keys[2], 2), own, number, TOK_DEV, E, TOP, CAP, 1))(expert_ids_keys, expert_ids_turns).reshape((TOKENS, TOP))
    route_weight = jnp.clip(0.019897461 + 0.27893066 * jax.random.uniform(keys[3], (TOKENS, TOP), jnp.float32) ** levels(keys[3], (TOKENS, TOP), ((0, 8),), -0.2, 0.2), 0.019897461, 0.29882812).astype(jnp.bfloat16)
    w_gate = normal_values(keys[4], (E, D, FFW), D ** -0.5, 0.125, ((0, 8), (1, 4)))
    w_up = normal_values(keys[5], (E, D, FFW), D ** -0.5, 0.125, ((0, 8), (1, 4)))
    w_down = normal_values(keys[6], (E, FFW, D), FFW ** -0.5, 0.25, ((0, 8), (2, 4)))
    return dict(tokens=tokens, out_grad=out_grad, expert_ids=expert_ids, route_weight=route_weight, w_gate=w_gate, w_up=w_up, w_down=w_down)


def hidden_terms(pre_gate, pre_up, pre_back, weight):
    sigmoid_gate = jax.nn.sigmoid(pre_gate)
    silu_gate = pre_gate * sigmoid_gate
    d_hidden = weight[..., None] * pre_back
    hidden = (silu_gate * pre_up).astype(jnp.bfloat16)
    gate_delta = (d_hidden * pre_up * sigmoid_gate * (1.0 + pre_gate * (1.0 - sigmoid_gate))).astype(jnp.bfloat16)
    up_delta = (d_hidden * silu_gate).astype(jnp.bfloat16)
    return hidden, gate_delta, up_delta


def quarter_sum(left_side, right_side, pattern):
    partials = jnp.einsum(pattern, left_side.astype(jnp.float32), right_side.astype(jnp.float32))
    rounded = lax.optimization_barrier(partials.astype(jnp.bfloat16))
    return jnp.sum(rounded.astype(jnp.float32), axis=0)


def reference(tokens, out_grad, expert_ids, route_weight, w_gate, w_up, w_down):
    token_count = tokens.shape[0]
    width = tokens.shape[1]
    quarter = width // N_REP
    column_rows = token_count // N_EP
    slot_rows = N_EP * CAP
    expert_range = jnp.arange(E, dtype=jnp.int32)
    matches = expert_ids[:, :, None] == expert_range[None, None, :]
    picked = jnp.sum(matches.astype(jnp.int32), axis=1).astype(jnp.int32).reshape(N_EP, column_rows, E)
    before = (jnp.cumsum(picked, axis=1).astype(jnp.int32) - picked).reshape(token_count, E)
    position = jnp.sum(jnp.where(matches, before[:, None, :], 0), axis=2).astype(jnp.int32)
    column = (jnp.arange(token_count, dtype=jnp.int32) // column_rows).astype(jnp.int32)[:, None]
    row_slot = (column * CAP + position).astype(jnp.int32)
    token_index = jnp.broadcast_to(jnp.arange(token_count, dtype=jnp.int32)[:, None], expert_ids.shape)
    pick_index = jnp.broadcast_to(jnp.arange(TOP, dtype=jnp.int32)[None, :], expert_ids.shape)
    slot_table = jnp.full((E, slot_rows), token_count, jnp.int32).at[expert_ids, row_slot].set(token_index)
    pick_table = jnp.zeros((E, slot_rows), jnp.int32).at[expert_ids, row_slot].set(pick_index)
    padded_tokens = jnp.concatenate([tokens, jnp.zeros((1, width), tokens.dtype)], axis=0)
    padded_grads = jnp.concatenate([out_grad, jnp.zeros((1, width), out_grad.dtype)], axis=0)
    padded_weight = jnp.concatenate([route_weight, jnp.zeros((1, TOP), route_weight.dtype)], axis=0)

    def per_expert(running, inputs):
        slot_tokens, slot_picks, gate_e, up_e, down_e = inputs
        rows_in = padded_tokens[slot_tokens]
        rows_grad = padded_grads[slot_tokens]
        weight = padded_weight[slot_tokens, slot_picks].astype(jnp.float32)
        split_in = rows_in.reshape(slot_rows, N_REP, quarter)
        split_grad = rows_grad.reshape(slot_rows, N_REP, quarter)
        pre_gate = quarter_sum(split_in, gate_e.reshape(N_REP, quarter, FFW), 'rqd,qdf->qrf')
        pre_up = quarter_sum(split_in, up_e.reshape(N_REP, quarter, FFW), 'rqd,qdf->qrf')
        pre_back = quarter_sum(split_grad, down_e.reshape(FFW, N_REP, quarter), 'rqd,fqd->qrf')
        hidden, gate_delta, up_delta = hidden_terms(pre_gate, pre_up, pre_back, weight)
        scaled_grad = (weight[:, None] * rows_grad.astype(jnp.float32)).astype(jnp.bfloat16)
        back_rows = jnp.dot(gate_delta, gate_e.T, preferred_element_type=jnp.float32)
        back_rows = back_rows + jnp.dot(up_delta, up_e.T, preferred_element_type=jnp.float32)
        back_rows = back_rows.astype(jnp.bfloat16)
        running = running.at[slot_tokens].add(back_rows.astype(jnp.float32))
        gate_grad = jnp.dot(rows_in.T, gate_delta, preferred_element_type=jnp.float32).astype(jnp.bfloat16)
        up_grad = jnp.dot(rows_in.T, up_delta, preferred_element_type=jnp.float32).astype(jnp.bfloat16)
        down_grad = jnp.dot(hidden.T, scaled_grad, preferred_element_type=jnp.float32).astype(jnp.bfloat16)
        return running, (gate_grad, up_grad, down_grad)

    start = jnp.zeros((token_count + 1, width), jnp.float32)
    token_sum, expert_grads = lax.scan(per_expert, start, (slot_table, pick_table, w_gate, w_up, w_down))
    token_grad = token_sum[:token_count].astype(jnp.bfloat16)
    return token_grad, expert_grads[0], expert_grads[1], expert_grads[2]
```

```python
import jax
import jax.numpy as jnp
from jax import lax
from jax.experimental import pallas as pl
from jax.experimental.pallas import tpu as pltpu
from jax.sharding import PartitionSpec as P

CAP = 9


def hidden_terms(pre_gate, pre_up, pre_back, weight):
    sigmoid_gate = jax.nn.sigmoid(pre_gate)
    silu_gate = pre_gate * sigmoid_gate
    d_hidden = weight[..., None] * pre_back
    hidden = (silu_gate * pre_up).astype(jnp.bfloat16)
    gate_delta = (
        d_hidden * pre_up * sigmoid_gate * (1.0 + pre_gate * (1.0 - sigmoid_gate))
    ).astype(jnp.bfloat16)
    up_delta = (d_hidden * silu_gate).astype(jnp.bfloat16)
    return (hidden, gate_delta, up_delta)


def body(tokens, out_grad, expert_ids, route_weight, w_gate, w_up, w_down):
    ep_ranks = lax.axis_size("ep")
    local_count = w_gate.shape[0]
    experts = local_count * ep_ranks
    quarter = tokens.shape[1]
    slot_rows = ep_ranks * CAP
    slot_total = experts * CAP
    expert_range = jnp.arange(experts, dtype=jnp.int32)
    matches = expert_ids[:, :, None] == expert_range[None, None, :]
    picked = jnp.sum(matches.astype(jnp.int32), axis=1)
    before = jnp.cumsum(picked, axis=0) - picked
    position = jnp.sum(jnp.where(matches, before[:, None, :], 0), axis=2)
    owner_col = expert_ids // local_count
    within = expert_ids % local_count
    slot_index = (within * ep_ranks + owner_col) * CAP + position
    select = slot_index[:, :, None] == jnp.arange(slot_total, dtype=jnp.int32)[None, None, :]
    placing = jnp.any(select, axis=1).astype(jnp.bfloat16)
    send_tokens = jnp.einsum("ts,td->sd", placing, tokens, preferred_element_type=jnp.float32)
    send_tokens = send_tokens.astype(jnp.bfloat16).reshape(local_count, ep_ranks, CAP, quarter)
    send_grads = jnp.einsum("ts,td->sd", placing, out_grad, preferred_element_type=jnp.float32)
    send_grads = send_grads.astype(jnp.bfloat16).reshape(local_count, ep_ranks, CAP, quarter)
    send_weight = jnp.sum(
        jnp.where(select, route_weight.astype(jnp.float32)[:, :, None], 0.0), axis=(0, 1)
    )
    send_weight = send_weight.astype(jnp.bfloat16).reshape(local_count, ep_ranks, CAP)
    routed_tokens, routed_grads, routed_weight = (
        lax.all_to_all(send_tokens, "ep", split_axis=1, concat_axis=1, tiled=True),
        lax.all_to_all(send_grads, "ep", split_axis=1, concat_axis=1, tiled=True),
        lax.all_to_all(send_weight, "ep", split_axis=1, concat_axis=1, tiled=True),
    )
    routed_tokens = routed_tokens.reshape(local_count, slot_rows, quarter)
    part_gate = jnp.einsum(
        "erd,edf->erf", routed_tokens, w_gate, preferred_element_type=jnp.float32
    )
    part_up = jnp.einsum("erd,edf->erf", routed_tokens, w_up, preferred_element_type=jnp.float32)
    routed_grads = routed_grads.reshape(local_count, slot_rows, quarter)
    part_back = jnp.einsum("erd,efd->erf", routed_grads, w_down, preferred_element_type=jnp.float32)
    weight = routed_weight.reshape(local_count, slot_rows).astype(jnp.float32)
    pre_gate, pre_up, pre_back = (
        lax.psum(part_gate.astype(jnp.bfloat16), "rep").astype(jnp.float32),
        lax.psum(part_up.astype(jnp.bfloat16), "rep").astype(jnp.float32),
        lax.psum(part_back.astype(jnp.bfloat16), "rep").astype(jnp.float32),
    )
    hidden, gate_delta, up_delta = hidden_terms(pre_gate, pre_up, pre_back, weight)
    scaled_grad = (weight[:, :, None] * routed_grads.astype(jnp.float32)).astype(jnp.bfloat16)
    back_rows = jnp.einsum("erf,edf->erd", gate_delta, w_gate, preferred_element_type=jnp.float32)
    back_rows = back_rows + jnp.einsum(
        "erf,edf->erd", up_delta, w_up, preferred_element_type=jnp.float32
    )
    back_rows = back_rows.astype(jnp.bfloat16).reshape(local_count, ep_ranks, CAP, quarter)
    returned = lax.all_to_all(back_rows, "ep", split_axis=1, concat_axis=1, tiled=True)
    grad_gate = jnp.einsum(
        "erd,erf->edf", routed_tokens, gate_delta, preferred_element_type=jnp.float32
    ).astype(jnp.bfloat16)
    grad_up = jnp.einsum(
        "erd,erf->edf", routed_tokens, up_delta, preferred_element_type=jnp.float32
    ).astype(jnp.bfloat16)
    grad_down = jnp.einsum(
        "erf,erd->efd", hidden, scaled_grad, preferred_element_type=jnp.float32
    ).astype(jnp.bfloat16)
    token_grad = jnp.einsum(
        "ts,sd->td",
        placing,
        returned.reshape(slot_total, quarter),
        preferred_element_type=jnp.float32,
    )
    return (token_grad.astype(jnp.bfloat16), grad_gate, grad_up, grad_down)


def routes(slot_row, slot_rows):
    rows = lax.broadcasted_iota(jnp.int32, (slot_rows, slot_row.shape[1]), 0)
    return rows == slot_row


def pre_kernel(slot_ref, tok_ref, wg_ref, wu_ref, wd_ref, *rest):
    rows_ref, part_ref = rest[-2:]
    slot_rows = rows_ref.shape[1]
    half = wg_ref.shape[1]
    ffw = wg_ref.shape[2]
    place = routes(slot_ref[0], slot_rows).astype(jnp.bfloat16)
    rows = jnp.dot(place, tok_ref[...], preferred_element_type=jnp.float32).astype(jnp.bfloat16)
    rows_ref[0] = rows
    gate = jnp.dot(rows[:, :half], wg_ref[0], preferred_element_type=jnp.float32)
    part_ref[0, :, :ffw] = gate.astype(jnp.bfloat16)
    up = jnp.dot(rows[:, :half], wu_ref[0], preferred_element_type=jnp.float32)
    part_ref[0, :, ffw : 2 * ffw] = up.astype(jnp.bfloat16)
    back = lax.dot_general(
        rows[:, half:], wd_ref[0], (((1,), (1,)), ((), ())), preferred_element_type=jnp.float32
    )
    part_ref[0, :, 2 * ffw :] = back.astype(jnp.bfloat16)


def post_kernel(slot_ref, weight_ref, rows_ref, sum_ref, wg_ref, wu_ref, *rest):
    acc_in, total_ref, gg_ref, gu_ref, gd_ref = rest[0], *rest[-4:]
    slot_rows = rows_ref.shape[1]
    half = wg_ref.shape[1]
    ffw = wg_ref.shape[2]
    hit = routes(slot_ref[0], slot_rows)
    weight = jnp.sum(jnp.where(hit, weight_ref[0], 0.0), axis=1, keepdims=True)
    place = hit.astype(jnp.bfloat16)
    pre_gate = sum_ref[0, :, :ffw].astype(jnp.float32)
    pre_up = sum_ref[0, :, ffw : 2 * ffw].astype(jnp.float32)
    pre_back = sum_ref[0, :, 2 * ffw :].astype(jnp.float32)
    sig = jax.nn.sigmoid(pre_gate)
    silu = pre_gate * sig
    d_hidden = weight * pre_back
    hidden = (silu * pre_up).astype(jnp.bfloat16)
    gate_delta = (d_hidden * pre_up * sig * (1.0 + pre_gate * (1.0 - sig))).astype(jnp.bfloat16)
    up_delta = (d_hidden * silu).astype(jnp.bfloat16)
    rows_in = rows_ref[0, :, :half]
    scaled = (weight * rows_ref[0, :, half:].astype(jnp.float32)).astype(jnp.bfloat16)
    nt = (((1,), (1,)), ((), ()))
    tn = (((0,), (0,)), ((), ()))
    f32 = jnp.float32
    back = lax.dot_general(gate_delta, wg_ref[0], nt, preferred_element_type=f32)
    back = back + lax.dot_general(up_delta, wu_ref[0], nt, preferred_element_type=f32)
    gg_ref[0] = lax.dot_general(rows_in, gate_delta, tn, preferred_element_type=f32).astype(
        jnp.bfloat16
    )
    gu_ref[0] = lax.dot_general(rows_in, up_delta, tn, preferred_element_type=f32).astype(
        jnp.bfloat16
    )
    gd_ref[0] = lax.dot_general(hidden, scaled, tn, preferred_element_type=f32).astype(jnp.bfloat16)

    @pl.when(pl.program_id(0) == 0)
    def _():
        total_ref[...] = acc_in[...]

    total_ref[...] += lax.dot_general(
        place, back.astype(jnp.bfloat16), tn, preferred_element_type=f32
    )


def pre_call(first, count, slot, gathered, w_gate, w_up, w_down, slot_rows, after):
    quarter, ffw = w_gate.shape[1:]
    token_count = slot.shape[2]
    mine = lambda i: (first + i, 0, 0)
    local = lambda i: (i, 0, 0)
    flops = 2 * count * slot_rows * quarter * (2 * token_count + 3 * ffw)
    return pl.pallas_call(
        pre_kernel,
        grid=(count,),
        in_specs=[
            pl.BlockSpec((1, 1, token_count), mine),
            pl.BlockSpec((token_count, 2 * quarter), lambda i: (0, 0)),
            pl.BlockSpec((1, quarter, ffw), mine),
            pl.BlockSpec((1, quarter, ffw), mine),
            pl.BlockSpec((1, ffw, quarter), mine),
        ]
        + [pl.BlockSpec(memory_space=pl.ANY)] * len(after),
        out_specs=[
            pl.BlockSpec((1, slot_rows, 2 * quarter), local),
            pl.BlockSpec((1, slot_rows, 3 * ffw), local),
        ],
        out_shape=[
            jax.ShapeDtypeStruct((count, slot_rows, 2 * quarter), jnp.bfloat16),
            jax.ShapeDtypeStruct((count, slot_rows, 3 * ffw), jnp.bfloat16),
        ],
        compiler_params=pltpu.CompilerParams(vmem_limit_bytes=32 << 20),
        cost_estimate=pl.CostEstimate(
            flops=flops, bytes_accessed=count * 6 * quarter * ffw, transcendentals=0
        ),
    )(slot, gathered, w_gate, w_up, w_down, *after)


def post_call(first, count, slot, weight, rows, summed, w_gate, w_up, total, grads):
    quarter, ffw = w_gate.shape[1:]
    local_count = w_gate.shape[0]
    token_count = slot.shape[2]
    slot_rows = rows.shape[1]
    mine = lambda i: (first + i, 0, 0)
    local = lambda i: (i, 0, 0)
    whole = lambda i: (0, 0)
    up_shape = jax.ShapeDtypeStruct((local_count, quarter, ffw), jnp.bfloat16)
    down_shape = jax.ShapeDtypeStruct((local_count, ffw, quarter), jnp.bfloat16)
    return pl.pallas_call(
        post_kernel,
        grid=(count,),
        in_specs=[
            pl.BlockSpec((1, 1, token_count), mine),
            pl.BlockSpec((1, 1, token_count), mine),
            pl.BlockSpec((1, slot_rows, 2 * quarter), local),
            pl.BlockSpec((1, slot_rows, 3 * ffw), local),
            pl.BlockSpec((1, quarter, ffw), mine),
            pl.BlockSpec((1, quarter, ffw), mine),
            pl.BlockSpec((token_count, quarter), whole),
        ]
        + [pl.BlockSpec(memory_space=pl.ANY)] * len(grads),
        out_specs=[
            pl.BlockSpec((token_count, quarter), whole),
            pl.BlockSpec((1, quarter, ffw), mine),
            pl.BlockSpec((1, quarter, ffw), mine),
            pl.BlockSpec((1, ffw, quarter), mine),
        ],
        out_shape=[
            jax.ShapeDtypeStruct((token_count, quarter), jnp.float32),
            up_shape,
            up_shape,
            down_shape,
        ],
        input_output_aliases={7 + i: 1 + i for i in range(len(grads))},
        compiler_params=pltpu.CompilerParams(vmem_limit_bytes=40 << 20),
        cost_estimate=pl.CostEstimate(
            flops=2 * count * slot_rows * quarter * (5 * ffw + token_count),
            bytes_accessed=count * 10 * quarter * ffw,
            transcendentals=0,
        ),
    )(slot, weight, rows, summed, w_gate, w_up, total, *grads)


CHUNKS = 4
LAG = 1


def gathered_body(tokens, out_grad, expert_ids, route_weight, w_gate, w_up, w_down):
    ep_ranks = lax.axis_size("ep")
    local_count, quarter, ffw = w_gate.shape
    experts = local_count * ep_ranks
    slot_rows = ep_ranks * CAP
    rows, picks = expert_ids.shape
    matches = expert_ids[:, :, None] == jnp.arange(experts, dtype=jnp.int32)[None, None, :]
    picked = jnp.sum(matches.astype(jnp.float32), axis=1).astype(jnp.bfloat16)
    earlier = jnp.tril(jnp.ones((rows, rows), jnp.bfloat16), -1)
    before = jnp.dot(earlier, picked, preferred_element_type=jnp.float32)
    position = jnp.sum(jnp.where(matches, before[:, None, :], 0.0), axis=2)
    facts = jnp.concatenate(
        [expert_ids.astype(jnp.bfloat16), position.astype(jnp.bfloat16), route_weight]
        + [jnp.zeros((rows, 128 - 3 * picks), jnp.bfloat16)],
        axis=1,
    )
    packed = jnp.concatenate([tokens, out_grad, facts], axis=1)
    everyone = lax.all_gather(packed, "ep", axis=0, tiled=True)
    token_count = rows * ep_ranks
    facts = everyone[:, 2 * quarter : 2 * quarter + 3 * picks].astype(jnp.float32).T
    column = (jnp.arange(token_count, dtype=jnp.int32) // rows).astype(jnp.float32)
    first = lax.axis_index("ep") * local_count
    mine = (first + jnp.arange(local_count, dtype=jnp.int32)).astype(jnp.float32)[:, None]
    slot = jnp.full((local_count, token_count), -1.0, jnp.float32)
    weight = jnp.zeros((local_count, token_count), jnp.float32)
    for k in range(picks):
        here = facts[k][None, :] == mine
        slot = jnp.where(here, (column * CAP + facts[picks + k])[None, :], slot)
        weight = jnp.where(here, facts[2 * picks + k][None, :], weight)
    slot = slot.astype(jnp.int32)[:, None, :]
    weight = weight[:, None, :]
    count = local_count // CHUNKS
    summed, routed = [], []
    for c in range(CHUNKS):
        after = summed[c - LAG : c - LAG + 1] if c >= LAG else []
        got, part = pre_call(
            c * count, count, slot, everyone, w_gate, w_up, w_down, slot_rows, after
        )
        routed.append(got)
        summed.append(lax.psum(part, "rep"))
    total, grads = jnp.zeros((token_count, quarter), jnp.float32), []
    for c in range(CHUNKS):
        total, *grads = post_call(
            c * count, count, slot, weight, routed[c], summed[c], w_gate, w_up, total, grads
        )
    token_grad = lax.psum_scatter(
        total.astype(jnp.bfloat16), "ep", scatter_dimension=0, tiled=True
    )
    return (token_grad, *grads)


def solution(mesh):
    placed = (
        P("ep", "rep"),
        P("ep", "rep"),
        P("ep", None),
        P("ep", None),
        P("ep", "rep", None),
        P("ep", "rep", None),
        P("ep", None, "rep"),
    )
    return jax.shard_map(
        gathered_body if mesh.shape["ep"] <= 8 else body,
        mesh=mesh,
        in_specs=placed,
        out_specs=(
            P("ep", "rep"),
            P("ep", "rep", None),
            P("ep", "rep", None),
            P("ep", None, "rep"),
        ),
        check_vma=False,
    )
```

```python
import jax
import jax.numpy as jnp
from jax import lax
from jax.experimental import pallas as pl
from jax.experimental.pallas import tpu as pltpu
from jax.sharding import PartitionSpec as P

CAP = 9


def hidden_terms(pre_gate, pre_up, pre_back, weight):
    sigmoid_gate = jax.nn.sigmoid(pre_gate)
    silu_gate = pre_gate * sigmoid_gate
    d_hidden = weight[..., None] * pre_back
    hidden = (silu_gate * pre_up).astype(jnp.bfloat16)
    gate_delta = (
        d_hidden * pre_up * sigmoid_gate * (1.0 + pre_gate * (1.0 - sigmoid_gate))
    ).astype(jnp.bfloat16)
    up_delta = (d_hidden * silu_gate).astype(jnp.bfloat16)
    return (hidden, gate_delta, up_delta)


def body(tokens, out_grad, expert_ids, route_weight, w_gate, w_up, w_down):
    ep_ranks = lax.axis_size("ep")
    local_count = w_gate.shape[0]
    experts = local_count * ep_ranks
    quarter = tokens.shape[1]
    slot_rows = ep_ranks * CAP
    slot_total = experts * CAP
    expert_range = jnp.arange(experts, dtype=jnp.int32)
    matches = expert_ids[:, :, None] == expert_range[None, None, :]
    picked = jnp.sum(matches.astype(jnp.int32), axis=1)
    before = jnp.cumsum(picked, axis=0) - picked
    position = jnp.sum(jnp.where(matches, before[:, None, :], 0), axis=2)
    owner_col = expert_ids // local_count
    within = expert_ids % local_count
    slot_index = (within * ep_ranks + owner_col) * CAP + position
    select = slot_index[:, :, None] == jnp.arange(slot_total, dtype=jnp.int32)[None, None, :]
    placing = jnp.any(select, axis=1).astype(jnp.bfloat16)
    send_tokens = jnp.einsum("ts,td->sd", placing, tokens, preferred_element_type=jnp.float32)
    send_tokens = send_tokens.astype(jnp.bfloat16).reshape(local_count, ep_ranks, CAP, quarter)
    send_grads = jnp.einsum("ts,td->sd", placing, out_grad, preferred_element_type=jnp.float32)
    send_grads = send_grads.astype(jnp.bfloat16).reshape(local_count, ep_ranks, CAP, quarter)
    send_weight = jnp.sum(
        jnp.where(select, route_weight.astype(jnp.float32)[:, :, None], 0.0), axis=(0, 1)
    )
    send_weight = send_weight.astype(jnp.bfloat16).reshape(local_count, ep_ranks, CAP)
    routed_tokens, routed_grads, routed_weight = (
        lax.all_to_all(send_tokens, "ep", split_axis=1, concat_axis=1, tiled=True),
        lax.all_to_all(send_grads, "ep", split_axis=1, concat_axis=1, tiled=True),
        lax.all_to_all(send_weight, "ep", split_axis=1, concat_axis=1, tiled=True),
    )
    routed_tokens = routed_tokens.reshape(local_count, slot_rows, quarter)
    part_gate = jnp.einsum(
        "erd,edf->erf", routed_tokens, w_gate, preferred_element_type=jnp.float32
    )
    part_up = jnp.einsum("erd,edf->erf", routed_tokens, w_up, preferred_element_type=jnp.float32)
    routed_grads = routed_grads.reshape(local_count, slot_rows, quarter)
    part_back = jnp.einsum("erd,efd->erf", routed_grads, w_down, preferred_element_type=jnp.float32)
    weight = routed_weight.reshape(local_count, slot_rows).astype(jnp.float32)
    pre_gate, pre_up, pre_back = (
        lax.psum(part_gate.astype(jnp.bfloat16), "rep").astype(jnp.float32),
        lax.psum(part_up.astype(jnp.bfloat16), "rep").astype(jnp.float32),
        lax.psum(part_back.astype(jnp.bfloat16), "rep").astype(jnp.float32),
    )
    hidden, gate_delta, up_delta = hidden_terms(pre_gate, pre_up, pre_back, weight)
    scaled_grad = (weight[:, :, None] * routed_grads.astype(jnp.float32)).astype(jnp.bfloat16)
    back_rows = jnp.einsum("erf,edf->erd", gate_delta, w_gate, preferred_element_type=jnp.float32)
    back_rows = back_rows + jnp.einsum(
        "erf,edf->erd", up_delta, w_up, preferred_element_type=jnp.float32
    )
    back_rows = back_rows.astype(jnp.bfloat16).reshape(local_count, ep_ranks, CAP, quarter)
    returned = lax.all_to_all(back_rows, "ep", split_axis=1, concat_axis=1, tiled=True)
    grad_gate = jnp.einsum(
        "erd,erf->edf", routed_tokens, gate_delta, preferred_element_type=jnp.float32
    ).astype(jnp.bfloat16)
    grad_up = jnp.einsum(
        "erd,erf->edf", routed_tokens, up_delta, preferred_element_type=jnp.float32
    ).astype(jnp.bfloat16)
    grad_down = jnp.einsum(
        "erf,erd->efd", hidden, scaled_grad, preferred_element_type=jnp.float32
    ).astype(jnp.bfloat16)
    token_grad = jnp.einsum(
        "ts,sd->td",
        placing,
        returned.reshape(slot_total, quarter),
        preferred_element_type=jnp.float32,
    )
    return (token_grad.astype(jnp.bfloat16), grad_gate, grad_up, grad_down)


def routes(slot_row, slot_rows):
    rows = lax.broadcasted_iota(jnp.int32, (slot_rows, slot_row.shape[1]), 0)
    return rows == slot_row


def pre_kernel(slot_ref, tok_ref, wg_ref, wu_ref, wd_ref, rows_ref, part_ref):
    slot_rows = rows_ref.shape[1]
    half = wg_ref.shape[1]
    ffw = wg_ref.shape[2]
    place = routes(slot_ref[0], slot_rows).astype(jnp.bfloat16)
    rows = jnp.dot(place, tok_ref[...], preferred_element_type=jnp.float32).astype(jnp.bfloat16)
    rows_ref[0] = rows
    gate = jnp.dot(rows[:, :half], wg_ref[0], preferred_element_type=jnp.float32)
    part_ref[0, :, :ffw] = gate.astype(jnp.bfloat16)
    up = jnp.dot(rows[:, :half], wu_ref[0], preferred_element_type=jnp.float32)
    part_ref[0, :, ffw : 2 * ffw] = up.astype(jnp.bfloat16)
    back = lax.dot_general(
        rows[:, half:], wd_ref[0], (((1,), (1,)), ((), ())), preferred_element_type=jnp.float32
    )
    part_ref[0, :, 2 * ffw :] = back.astype(jnp.bfloat16)


def deltas(slot_ref, weight_ref, sum_ref, slot_rows, ffw):
    hit = routes(slot_ref[0], slot_rows)
    weight = jnp.sum(jnp.where(hit, weight_ref[0], 0.0), axis=1, keepdims=True)
    pre_gate = sum_ref[0, :, :ffw].astype(jnp.float32)
    pre_up = sum_ref[0, :, ffw : 2 * ffw].astype(jnp.float32)
    pre_back = sum_ref[0, :, 2 * ffw :].astype(jnp.float32)
    sig = jax.nn.sigmoid(pre_gate)
    silu = pre_gate * sig
    d_hidden = weight * pre_back
    hidden = (silu * pre_up).astype(jnp.bfloat16)
    gate_delta = (d_hidden * pre_up * sig * (1.0 + pre_gate * (1.0 - sig))).astype(jnp.bfloat16)
    up_delta = (d_hidden * silu).astype(jnp.bfloat16)
    return hit, weight, hidden, gate_delta, up_delta


NT = (((1,), (1,)), ((), ()))
TN = (((0,), (0,)), ((), ()))


def back_kernel(slot_ref, weight_ref, sum_ref, wg_ref, wu_ref, out_ref, total_ref):
    ffw = wg_ref.shape[2]
    hit, _, _, gate_delta, up_delta = deltas(slot_ref, weight_ref, sum_ref, sum_ref.shape[1], ffw)
    f32 = jnp.float32
    back = lax.dot_general(gate_delta, wg_ref[0], NT, preferred_element_type=f32)
    back = back + lax.dot_general(up_delta, wu_ref[0], NT, preferred_element_type=f32)
    place = hit.astype(jnp.bfloat16)
    mine = lax.dot_general(place, back.astype(jnp.bfloat16), TN, preferred_element_type=f32)

    @pl.when(pl.program_id(0) == 0)
    def _():
        total_ref[...] = mine

    @pl.when(pl.program_id(0) > 0)
    def _():
        total_ref[...] += mine

    @pl.when(pl.program_id(0) == pl.num_programs(0) - 1)
    def _():
        out_ref[...] = total_ref[...].astype(jnp.bfloat16)


def grad_kernel(slot_ref, weight_ref, rows_ref, sum_ref, gg_ref, gu_ref, gd_ref):
    half, ffw = gg_ref.shape[1:]
    _, weight, hidden, gate_delta, up_delta = deltas(
        slot_ref, weight_ref, sum_ref, rows_ref.shape[1], ffw
    )
    rows_in = rows_ref[0, :, :half]
    scaled = (weight * rows_ref[0, :, half:].astype(jnp.float32)).astype(jnp.bfloat16)
    f32, b16 = jnp.float32, jnp.bfloat16
    gg_ref[0] = lax.dot_general(rows_in, gate_delta, TN, preferred_element_type=f32).astype(b16)
    gu_ref[0] = lax.dot_general(rows_in, up_delta, TN, preferred_element_type=f32).astype(b16)
    gd_ref[0] = lax.dot_general(hidden, scaled, TN, preferred_element_type=f32).astype(b16)


def pre_call(slot, gathered, w_gate, w_up, w_down, slot_rows):
    count, quarter, ffw = w_gate.shape
    token_count = slot.shape[2]
    mine = lambda i: (i, 0, 0)
    flops = 2 * count * slot_rows * quarter * (2 * token_count + 3 * ffw)
    return pl.pallas_call(
        pre_kernel,
        grid=(count,),
        in_specs=[
            pl.BlockSpec((1, 1, token_count), mine),
            pl.BlockSpec((token_count, 2 * quarter), lambda i: (0, 0)),
            pl.BlockSpec((1, quarter, ffw), mine),
            pl.BlockSpec((1, quarter, ffw), mine),
            pl.BlockSpec((1, ffw, quarter), mine),
        ],
        out_specs=[
            pl.BlockSpec((1, slot_rows, 2 * quarter), mine),
            pl.BlockSpec((1, slot_rows, 3 * ffw), mine),
        ],
        out_shape=[
            jax.ShapeDtypeStruct((count, slot_rows, 2 * quarter), jnp.bfloat16),
            jax.ShapeDtypeStruct((count, slot_rows, 3 * ffw), jnp.bfloat16),
        ],
        compiler_params=pltpu.CompilerParams(vmem_limit_bytes=32 << 20),
        cost_estimate=pl.CostEstimate(
            flops=flops, bytes_accessed=count * 6 * quarter * ffw, transcendentals=0
        ),
    )(slot, gathered, w_gate, w_up, w_down)


def back_call(slot, weight, summed, w_gate, w_up):
    local_count, quarter, ffw = w_gate.shape
    token_count = slot.shape[2]
    slot_rows = summed.shape[1]
    mine = lambda i: (i, 0, 0)
    return pl.pallas_call(
        back_kernel,
        grid=(local_count,),
        in_specs=[
            pl.BlockSpec((1, 1, token_count), mine),
            pl.BlockSpec((1, 1, token_count), mine),
            pl.BlockSpec((1, slot_rows, 3 * ffw), mine),
            pl.BlockSpec((1, quarter, ffw), mine),
            pl.BlockSpec((1, quarter, ffw), mine),
        ],
        out_specs=pl.BlockSpec((token_count, quarter), lambda i: (0, 0)),
        out_shape=jax.ShapeDtypeStruct((token_count, quarter), jnp.bfloat16),
        scratch_shapes=[pltpu.VMEM((token_count, quarter), jnp.float32)],
        compiler_params=pltpu.CompilerParams(vmem_limit_bytes=32 << 20),
        cost_estimate=pl.CostEstimate(
            flops=2 * local_count * slot_rows * quarter * (2 * ffw + token_count),
            bytes_accessed=local_count * 4 * quarter * ffw,
            transcendentals=0,
        ),
    )(slot, weight, summed, w_gate, w_up)


def grad_call(slot, weight, rows, summed, quarter, ffw):
    local_count, _, token_count = slot.shape
    slot_rows = rows.shape[1]
    mine = lambda i: (i, 0, 0)
    up_shape = jax.ShapeDtypeStruct((local_count, quarter, ffw), jnp.bfloat16)
    down_shape = jax.ShapeDtypeStruct((local_count, ffw, quarter), jnp.bfloat16)
    return pl.pallas_call(
        grad_kernel,
        grid=(local_count,),
        in_specs=[
            pl.BlockSpec((1, 1, token_count), mine),
            pl.BlockSpec((1, 1, token_count), mine),
            pl.BlockSpec((1, slot_rows, 2 * quarter), mine),
            pl.BlockSpec((1, slot_rows, 3 * ffw), mine),
        ],
        out_specs=[
            pl.BlockSpec((1, quarter, ffw), mine),
            pl.BlockSpec((1, quarter, ffw), mine),
            pl.BlockSpec((1, ffw, quarter), mine),
        ],
        out_shape=[up_shape, up_shape, down_shape],
        compiler_params=pltpu.CompilerParams(vmem_limit_bytes=32 << 20),
        cost_estimate=pl.CostEstimate(
            flops=6 * local_count * slot_rows * quarter * ffw,
            bytes_accessed=local_count * 6 * quarter * ffw,
            transcendentals=0,
        ),
    )(slot, weight, rows, summed)


def gathered_body(tokens, out_grad, expert_ids, route_weight, w_gate, w_up, w_down):
    ep_ranks = lax.axis_size("ep")
    local_count, quarter, ffw = w_gate.shape
    experts = local_count * ep_ranks
    slot_rows = ep_ranks * CAP
    rows, picks = expert_ids.shape
    matches = expert_ids[:, :, None] == jnp.arange(experts, dtype=jnp.int32)[None, None, :]
    picked = jnp.sum(matches.astype(jnp.float32), axis=1).astype(jnp.bfloat16)
    earlier = jnp.tril(jnp.ones((rows, rows), jnp.bfloat16), -1)
    before = jnp.dot(earlier, picked, preferred_element_type=jnp.float32)
    position = jnp.sum(jnp.where(matches, before[:, None, :], 0.0), axis=2)
    facts = jnp.concatenate(
        [expert_ids.astype(jnp.bfloat16), position.astype(jnp.bfloat16), route_weight]
        + [jnp.zeros((rows, 128 - 3 * picks), jnp.bfloat16)],
        axis=1,
    )
    packed = jnp.concatenate([tokens, out_grad, facts], axis=1)
    everyone = lax.all_gather(packed, "ep", axis=0, tiled=True)
    token_count = rows * ep_ranks
    facts = everyone[:, 2 * quarter : 2 * quarter + 3 * picks].astype(jnp.float32).T
    column = (jnp.arange(token_count, dtype=jnp.int32) // rows).astype(jnp.float32)
    first = lax.axis_index("ep") * local_count
    mine = (first + jnp.arange(local_count, dtype=jnp.int32)).astype(jnp.float32)[:, None]
    slot = jnp.full((local_count, token_count), -1.0, jnp.float32)
    weight = jnp.zeros((local_count, token_count), jnp.float32)
    for k in range(picks):
        here = facts[k][None, :] == mine
        slot = jnp.where(here, (column * CAP + facts[picks + k])[None, :], slot)
        weight = jnp.where(here, facts[2 * picks + k][None, :], weight)
    slot = slot.astype(jnp.int32)[:, None, :]
    weight = weight[:, None, :]
    routed, part = pre_call(slot, everyone, w_gate, w_up, w_down, slot_rows)
    summed = lax.psum(part, "rep")
    total = back_call(slot, weight, summed, w_gate, w_up)
    token_grad = lax.psum_scatter(total, "ep", scatter_dimension=0, tiled=True)
    return (token_grad, *grad_call(slot, weight, routed, summed, quarter, ffw))


def solution(mesh):
    placed = (
        P("ep", "rep"),
        P("ep", "rep"),
        P("ep", None),
        P("ep", None),
        P("ep", "rep", None),
        P("ep", "rep", None),
        P("ep", None, "rep"),
    )
    return jax.shard_map(
        gathered_body if mesh.shape["ep"] <= 8 else body,
        mesh=mesh,
        in_specs=placed,
        out_specs=(
            P("ep", "rep"),
            P("ep", "rep", None),
            P("ep", "rep", None),
            P("ep", None, "rep"),
        ),
        check_vma=False,
    )
```

```python
import jax
import jax.numpy as jnp
from jax import lax
from jax.experimental import pallas as pl
from jax.experimental.pallas import tpu as pltpu
from jax.sharding import PartitionSpec as P

CAP = 9


def hidden_terms(pre_gate, pre_up, pre_back, weight):
    sigmoid_gate = jax.nn.sigmoid(pre_gate)
    silu_gate = pre_gate * sigmoid_gate
    d_hidden = weight[..., None] * pre_back
    hidden = (silu_gate * pre_up).astype(jnp.bfloat16)
    gate_delta = (
        d_hidden * pre_up * sigmoid_gate * (1.0 + pre_gate * (1.0 - sigmoid_gate))
    ).astype(jnp.bfloat16)
    up_delta = (d_hidden * silu_gate).astype(jnp.bfloat16)
    return (hidden, gate_delta, up_delta)


def body(tokens, out_grad, expert_ids, route_weight, w_gate, w_up, w_down):
    ep_ranks = lax.axis_size("ep")
    local_count = w_gate.shape[0]
    experts = local_count * ep_ranks
    quarter = tokens.shape[1]
    slot_rows = ep_ranks * CAP
    slot_total = experts * CAP
    expert_range = jnp.arange(experts, dtype=jnp.int32)
    matches = expert_ids[:, :, None] == expert_range[None, None, :]
    picked = jnp.sum(matches.astype(jnp.int32), axis=1)
    before = jnp.cumsum(picked, axis=0) - picked
    position = jnp.sum(jnp.where(matches, before[:, None, :], 0), axis=2)
    owner_col = expert_ids // local_count
    within = expert_ids % local_count
    slot_index = (within * ep_ranks + owner_col) * CAP + position
    select = slot_index[:, :, None] == jnp.arange(slot_total, dtype=jnp.int32)[None, None, :]
    placing = jnp.any(select, axis=1).astype(jnp.bfloat16)
    send_tokens = jnp.einsum("ts,td->sd", placing, tokens, preferred_element_type=jnp.float32)
    send_tokens = send_tokens.astype(jnp.bfloat16).reshape(local_count, ep_ranks, CAP, quarter)
    send_grads = jnp.einsum("ts,td->sd", placing, out_grad, preferred_element_type=jnp.float32)
    send_grads = send_grads.astype(jnp.bfloat16).reshape(local_count, ep_ranks, CAP, quarter)
    send_weight = jnp.sum(
        jnp.where(select, route_weight.astype(jnp.float32)[:, :, None], 0.0), axis=(0, 1)
    )
    send_weight = send_weight.astype(jnp.bfloat16).reshape(local_count, ep_ranks, CAP)
    routed_tokens, routed_grads, routed_weight = (
        lax.all_to_all(send_tokens, "ep", split_axis=1, concat_axis=1, tiled=True),
        lax.all_to_all(send_grads, "ep", split_axis=1, concat_axis=1, tiled=True),
        lax.all_to_all(send_weight, "ep", split_axis=1, concat_axis=1, tiled=True),
    )
    routed_tokens = routed_tokens.reshape(local_count, slot_rows, quarter)
    part_gate = jnp.einsum(
        "erd,edf->erf", routed_tokens, w_gate, preferred_element_type=jnp.float32
    )
    part_up = jnp.einsum("erd,edf->erf", routed_tokens, w_up, preferred_element_type=jnp.float32)
    routed_grads = routed_grads.reshape(local_count, slot_rows, quarter)
    part_back = jnp.einsum("erd,efd->erf", routed_grads, w_down, preferred_element_type=jnp.float32)
    weight = routed_weight.reshape(local_count, slot_rows).astype(jnp.float32)
    pre_gate, pre_up, pre_back = (
        lax.psum(part_gate.astype(jnp.bfloat16), "rep").astype(jnp.float32),
        lax.psum(part_up.astype(jnp.bfloat16), "rep").astype(jnp.float32),
        lax.psum(part_back.astype(jnp.bfloat16), "rep").astype(jnp.float32),
    )
    hidden, gate_delta, up_delta = hidden_terms(pre_gate, pre_up, pre_back, weight)
    scaled_grad = (weight[:, :, None] * routed_grads.astype(jnp.float32)).astype(jnp.bfloat16)
    back_rows = jnp.einsum("erf,edf->erd", gate_delta, w_gate, preferred_element_type=jnp.float32)
    back_rows = back_rows + jnp.einsum(
        "erf,edf->erd", up_delta, w_up, preferred_element_type=jnp.float32
    )
    back_rows = back_rows.astype(jnp.bfloat16).reshape(local_count, ep_ranks, CAP, quarter)
    returned = lax.all_to_all(back_rows, "ep", split_axis=1, concat_axis=1, tiled=True)
    grad_gate = jnp.einsum(
        "erd,erf->edf", routed_tokens, gate_delta, preferred_element_type=jnp.float32
    ).astype(jnp.bfloat16)
    grad_up = jnp.einsum(
        "erd,erf->edf", routed_tokens, up_delta, preferred_element_type=jnp.float32
    ).astype(jnp.bfloat16)
    grad_down = jnp.einsum(
        "erf,erd->efd", hidden, scaled_grad, preferred_element_type=jnp.float32
    ).astype(jnp.bfloat16)
    token_grad = jnp.einsum(
        "ts,sd->td",
        placing,
        returned.reshape(slot_total, quarter),
        preferred_element_type=jnp.float32,
    )
    return (token_grad.astype(jnp.bfloat16), grad_gate, grad_up, grad_down)


def routes(slot_row, slot_rows):
    rows = lax.broadcasted_iota(jnp.int32, (slot_rows, slot_row.shape[1]), 0)
    return rows == slot_row


def pre_kernel(slot_ref, tok_ref, wg_ref, wu_ref, wd_ref, rows_ref, part_ref):
    slot_rows = rows_ref.shape[1]
    half = wg_ref.shape[1]
    ffw = wg_ref.shape[2]
    place = routes(slot_ref[0], slot_rows).astype(jnp.bfloat16)
    rows = jnp.dot(place, tok_ref[...], preferred_element_type=jnp.float32).astype(jnp.bfloat16)
    rows_ref[0] = rows
    gate = jnp.dot(rows[:, :half], wg_ref[0], preferred_element_type=jnp.float32)
    part_ref[0, :, :ffw] = gate.astype(jnp.bfloat16)
    up = jnp.dot(rows[:, :half], wu_ref[0], preferred_element_type=jnp.float32)
    part_ref[0, :, ffw : 2 * ffw] = up.astype(jnp.bfloat16)
    back = lax.dot_general(
        rows[:, half:], wd_ref[0], (((1,), (1,)), ((), ())), preferred_element_type=jnp.float32
    )
    part_ref[0, :, 2 * ffw :] = back.astype(jnp.bfloat16)


def deltas(slot_ref, weight_ref, sum_ref, slot_rows, ffw):
    hit = routes(slot_ref[0], slot_rows)
    weight = jnp.sum(jnp.where(hit, weight_ref[0], 0.0), axis=1, keepdims=True)
    pre_gate = sum_ref[0, :, :ffw].astype(jnp.float32)
    pre_up = sum_ref[0, :, ffw : 2 * ffw].astype(jnp.float32)
    pre_back = sum_ref[0, :, 2 * ffw :].astype(jnp.float32)
    sig = jax.nn.sigmoid(pre_gate)
    silu = pre_gate * sig
    d_hidden = weight * pre_back
    hidden = (silu * pre_up).astype(jnp.bfloat16)
    gate_delta = (d_hidden * pre_up * sig * (1.0 + pre_gate * (1.0 - sig))).astype(jnp.bfloat16)
    up_delta = (d_hidden * silu).astype(jnp.bfloat16)
    return hit, weight, hidden, gate_delta, up_delta


NT = (((1,), (1,)), ((), ()))
TN = (((0,), (0,)), ((), ()))


def back_kernel(slot_ref, weight_ref, sum_ref, wg_ref, wu_ref, out_ref, total_ref):
    ffw = wg_ref.shape[2]
    hit, _, _, gate_delta, up_delta = deltas(slot_ref, weight_ref, sum_ref, sum_ref.shape[1], ffw)
    f32 = jnp.float32
    back = lax.dot_general(gate_delta, wg_ref[0], NT, preferred_element_type=f32)
    back = back + lax.dot_general(up_delta, wu_ref[0], NT, preferred_element_type=f32)
    place = hit.astype(jnp.bfloat16)
    mine = lax.dot_general(place, back.astype(jnp.bfloat16), TN, preferred_element_type=f32)

    @pl.when(pl.program_id(0) == 0)
    def _():
        total_ref[...] = mine

    @pl.when(pl.program_id(0) > 0)
    def _():
        total_ref[...] += mine

    @pl.when(pl.program_id(0) == pl.num_programs(0) - 1)
    def _():
        out_ref[...] = total_ref[...].astype(jnp.bfloat16)


def grad_kernel(slot_ref, weight_ref, rows_ref, sum_ref, gg_ref, gu_ref, gd_ref):
    half, ffw = gg_ref.shape[1:]
    _, weight, hidden, gate_delta, up_delta = deltas(
        slot_ref, weight_ref, sum_ref, rows_ref.shape[1], ffw
    )
    rows_in = rows_ref[0, :, :half]
    scaled = (weight * rows_ref[0, :, half:].astype(jnp.float32)).astype(jnp.bfloat16)
    f32, b16 = jnp.float32, jnp.bfloat16
    gg_ref[0] = lax.dot_general(rows_in, gate_delta, TN, preferred_element_type=f32).astype(b16)
    gu_ref[0] = lax.dot_general(rows_in, up_delta, TN, preferred_element_type=f32).astype(b16)
    gd_ref[0] = lax.dot_general(hidden, scaled, TN, preferred_element_type=f32).astype(b16)


def pre_call(slot, gathered, w_gate, w_up, w_down, slot_rows):
    count, quarter, ffw = w_gate.shape
    token_count = slot.shape[2]
    mine = lambda i: (i, 0, 0)
    flops = 2 * count * slot_rows * quarter * (2 * token_count + 3 * ffw)
    return pl.pallas_call(
        pre_kernel,
        grid=(count,),
        in_specs=[
            pl.BlockSpec((1, 1, token_count), mine),
            pl.BlockSpec((token_count, 2 * quarter), lambda i: (0, 0)),
            pl.BlockSpec((1, quarter, ffw), mine),
            pl.BlockSpec((1, quarter, ffw), mine),
            pl.BlockSpec((1, ffw, quarter), mine),
        ],
        out_specs=[
            pl.BlockSpec((1, slot_rows, 2 * quarter), mine),
            pl.BlockSpec((1, slot_rows, 3 * ffw), mine),
        ],
        out_shape=[
            jax.ShapeDtypeStruct((count, slot_rows, 2 * quarter), jnp.bfloat16),
            jax.ShapeDtypeStruct((count, slot_rows, 3 * ffw), jnp.bfloat16),
        ],
        compiler_params=pltpu.CompilerParams(vmem_limit_bytes=32 << 20),
        cost_estimate=pl.CostEstimate(
            flops=flops, bytes_accessed=count * 6 * quarter * ffw, transcendentals=0
        ),
    )(slot, gathered, w_gate, w_up, w_down)


def back_call(slot, weight, summed, w_gate, w_up):
    local_count, quarter, ffw = w_gate.shape
    token_count = slot.shape[2]
    slot_rows = summed.shape[1]
    mine = lambda i: (i, 0, 0)
    return pl.pallas_call(
        back_kernel,
        grid=(local_count,),
        in_specs=[
            pl.BlockSpec((1, 1, token_count), mine),
            pl.BlockSpec((1, 1, token_count), mine),
            pl.BlockSpec((1, slot_rows, 3 * ffw), mine),
            pl.BlockSpec((1, quarter, ffw), mine),
            pl.BlockSpec((1, quarter, ffw), mine),
        ],
        out_specs=pl.BlockSpec((token_count, quarter), lambda i: (0, 0)),
        out_shape=jax.ShapeDtypeStruct((token_count, quarter), jnp.bfloat16),
        scratch_shapes=[pltpu.VMEM((token_count, quarter), jnp.float32)],
        compiler_params=pltpu.CompilerParams(vmem_limit_bytes=32 << 20),
        cost_estimate=pl.CostEstimate(
            flops=2 * local_count * slot_rows * quarter * (2 * ffw + token_count),
            bytes_accessed=local_count * 4 * quarter * ffw,
            transcendentals=0,
        ),
    )(slot, weight, summed, w_gate, w_up)


def grad_call(slot, weight, rows, summed, quarter, ffw):
    local_count, _, token_count = slot.shape
    slot_rows = rows.shape[1]
    mine = lambda i: (i, 0, 0)
    up_shape = jax.ShapeDtypeStruct((local_count, quarter, ffw), jnp.bfloat16)
    down_shape = jax.ShapeDtypeStruct((local_count, ffw, quarter), jnp.bfloat16)
    return pl.pallas_call(
        grad_kernel,
        grid=(local_count,),
        in_specs=[
            pl.BlockSpec((1, 1, token_count), mine),
            pl.BlockSpec((1, 1, token_count), mine),
            pl.BlockSpec((1, slot_rows, 2 * quarter), mine),
            pl.BlockSpec((1, slot_rows, 3 * ffw), mine),
        ],
        out_specs=[
            pl.BlockSpec((1, quarter, ffw), mine),
            pl.BlockSpec((1, quarter, ffw), mine),
            pl.BlockSpec((1, ffw, quarter), mine),
        ],
        out_shape=[up_shape, up_shape, down_shape],
        compiler_params=pltpu.CompilerParams(vmem_limit_bytes=32 << 20),
        cost_estimate=pl.CostEstimate(
            flops=6 * local_count * slot_rows * quarter * ffw,
            bytes_accessed=local_count * 6 * quarter * ffw,
            transcendentals=0,
        ),
    )(slot, weight, rows, summed)


def swap(value, bit):
    return lax.ppermute(value, "rep", [(r, r ^ bit) for r in range(lax.axis_size("rep"))])


def halves(value, side):
    pair = value.reshape((2, value.shape[0] // 2) + value.shape[1:])
    return (
        lax.dynamic_index_in_dim(pair, side, 0, keepdims=False),
        lax.dynamic_index_in_dim(pair, 1 - side, 0, keepdims=False),
    )


def added(kept, came):
    return (kept.astype(jnp.float32) + came.astype(jnp.float32)).astype(jnp.bfloat16)


def joined(kept, came, side):
    low = jnp.where(side == 0, kept, came)
    return jnp.concatenate([low, jnp.where(side == 0, came, kept)], axis=0)


def rep_sum(part):
    rank = lax.axis_index("rep")
    sides = {1: rank % 2, 2: rank // 2}
    count = part.shape[0] // 2
    paths = [(part[:count], (1, 2)), (part[count:], (2, 1))]
    values = [value for value, _ in paths]
    for step in (0, 1):
        split = [halves(v, sides[order[step]]) for v, (_, order) in zip(values, paths)]
        came = [swap(other, order[step]) for (_, other), (_, order) in zip(split, paths)]
        values = [added(kept, new) for (kept, _), new in zip(split, came)]
    for step in (1, 0):
        came = [swap(v, order[step]) for v, (_, order) in zip(values, paths)]
        values = [
            joined(v, new, sides[order[step]]) for v, new, (_, order) in zip(values, came, paths)
        ]
    return jnp.concatenate(values, axis=0)


def gathered_body(tokens, out_grad, expert_ids, route_weight, w_gate, w_up, w_down):
    ep_ranks = lax.axis_size("ep")
    local_count, quarter, ffw = w_gate.shape
    experts = local_count * ep_ranks
    slot_rows = ep_ranks * CAP
    rows, picks = expert_ids.shape
    matches = expert_ids[:, :, None] == jnp.arange(experts, dtype=jnp.int32)[None, None, :]
    picked = jnp.sum(matches.astype(jnp.float32), axis=1).astype(jnp.bfloat16)
    earlier = jnp.tril(jnp.ones((rows, rows), jnp.bfloat16), -1)
    before = jnp.dot(earlier, picked, preferred_element_type=jnp.float32)
    position = jnp.sum(jnp.where(matches, before[:, None, :], 0.0), axis=2)
    facts = jnp.concatenate(
        [expert_ids.astype(jnp.bfloat16), position.astype(jnp.bfloat16), route_weight]
        + [jnp.zeros((rows, 128 - 3 * picks), jnp.bfloat16)],
        axis=1,
    )
    packed = jnp.concatenate([tokens, out_grad, facts], axis=1)
    everyone = lax.all_gather(packed, "ep", axis=0, tiled=True)
    token_count = rows * ep_ranks
    facts = everyone[:, 2 * quarter : 2 * quarter + 3 * picks].astype(jnp.float32).T
    column = (jnp.arange(token_count, dtype=jnp.int32) // rows).astype(jnp.float32)
    first = lax.axis_index("ep") * local_count
    mine = (first + jnp.arange(local_count, dtype=jnp.int32)).astype(jnp.float32)[:, None]
    slot = jnp.full((local_count, token_count), -1.0, jnp.float32)
    weight = jnp.zeros((local_count, token_count), jnp.float32)
    for k in range(picks):
        here = facts[k][None, :] == mine
        slot = jnp.where(here, (column * CAP + facts[picks + k])[None, :], slot)
        weight = jnp.where(here, facts[2 * picks + k][None, :], weight)
    slot = slot.astype(jnp.int32)[:, None, :]
    weight = weight[:, None, :]
    routed, part = pre_call(slot, everyone, w_gate, w_up, w_down, slot_rows)
    summed = rep_sum(part)
    total = back_call(slot, weight, summed, w_gate, w_up)
    token_grad = lax.psum_scatter(total, "ep", scatter_dimension=0, tiled=True)
    return (token_grad, *grad_call(slot, weight, routed, summed, quarter, ffw))


def solution(mesh):
    placed = (
        P("ep", "rep"),
        P("ep", "rep"),
        P("ep", None),
        P("ep", None),
        P("ep", "rep", None),
        P("ep", "rep", None),
        P("ep", None, "rep"),
    )
    return jax.shard_map(
        gathered_body if mesh.shape["ep"] <= 8 and mesh.shape["rep"] == 4 else body,
        mesh=mesh,
        in_specs=placed,
        out_specs=(
            P("ep", "rep"),
            P("ep", "rep", None),
            P("ep", "rep", None),
            P("ep", None, "rep"),
        ),
        check_vma=False,
    )
```
